256 devices in a mesh: dp: 64 (over x, z, core), tensor: 4 (over y).
Axes of the slice: x: 4, y: 4, z: 8, core: 2. Of those that a mesh axis runs over, the one named last changes fastest.
Arguments:
- tokens: bfloat16 [131072, 2560], P('dp'), may hold values from -6 to 6
- upstream: bfloat16 [131072, 2560], P('dp', 'tensor'), may hold values from -0.19921875 to 0.19921875
- memory: bfloat16 [64, 2560, 2560], P('dp', None, 'tensor'), may hold values from -3 to 3
- block_lists: int32 [64, 4, 1024], P('dp', 'tensor'), may hold values from 0 to 12799, as said below
- leader: int32 [1], replicated, may hold values from 0 to 63
Outputs:
- summed: float32 [4, 1024, 128], P('tensor')
- memory_out: bfloat16 [64, 2560, 2560], P('dp', None, 'tensor')
The draws below stay inside these ranges and needn't reach their ends.
Inputs may be any that keep to these rules, and one draw needn't show every extreme that they name: `block_lists`: each row lists 1024 distinct block numbers in increasing order, always including 0 and 12799.
All inputs are finite; a program needn't handle non-finite values.
Results may differ from the reference program's by a relative error of at most 0.001.
Values sent between devices are 32-bit elements; how exact they have to be, the bound alone decides.
A program may use at most 128 MiB of HBM per device.

```python
import jax
import jax.numpy as jnp
from jax import lax

FEAT = 2560
HEADS = 20
HD = 128
TOK_DEV = 2048
K = 1024
NBLK = 12800
TOKENS = 131072
N_DP = 64
N_TENSOR = 4


def draw_block_lists(key, part):
    key = jax.random.fold_in(key, 7)
    keys = jax.random.split(key, N_DP * N_TENSOR)

    def single(row_key):
        inner = jax.random.permutation(row_key, NBLK - 2)[:K - 2].astype(jnp.int32) + 1
        ends = jnp.array([0, NBLK - 1], dtype=jnp.int32)
        return jnp.sort(jnp.concatenate([ends, inner]))
    return jax.vmap(single)(keys).reshape(N_DP, N_TENSOR, K).astype(jnp.int32)


def steps_of(rng, dims, cuts, smallest, largest):
    factor_of, own = 1.0, jax.random.fold_in(rng, 6)
    for axis_at, parts in cuts:
        steps = jnp.exp(jax.random.uniform(jax.random.fold_in(own, axis_at), (parts,), jnp.float32, smallest / len(cuts), largest / len(cuts)))
        factor_of = factor_of * jnp.repeat(steps, dims[axis_at] // parts).reshape([-1 if axis == axis_at else 1 for axis in range(len(dims))])
    return factor_of


def scatter_about(key, extent, spread, most, cuts=(), held_as=jnp.bfloat16):
    loudness = steps_of(key, extent, cuts, -0.22, 0.18) if cuts else 1.0
    result = jax.random.normal(key, extent, jnp.float32) * spread * loudness
    return jnp.minimum(jnp.maximum(result, -most), most).astype(held_as)


def setup_inputs(seed: int = 0) -> dict:
    arg_keys = jax.random.split(jax.random.key(seed), 6)
    tokens = scatter_about(arg_keys[0], (TOKENS, FEAT), 1.0, 6.0, ((0, 64),))
    upstream = scatter_about(arg_keys[1], (TOKENS, HEADS * HD), 0.03125, 0.19921875, ((0, 64), (1, 4)))
    memory = scatter_about(arg_keys[2], (N_DP, FEAT, HEADS * HD), 0.5, 3.0, ((0, 64), (2, 4)))
    block_lists = draw_block_lists(jax.random.fold_in(arg_keys[5], 71), 0)
    leader = jax.random.randint(arg_keys[4], (1,), 0, N_DP).astype(jnp.int32)
    return dict(tokens=tokens, upstream=upstream, memory=memory, block_lists=block_lists, leader=leader)


LOWPASS = 0.3


def reference(tokens, upstream, memory, block_lists, leader):
    heads_here = HEADS // N_TENSOR
    chosen = block_lists[leader[0]]
    shard_ids = jnp.arange(N_TENSOR, dtype=jnp.int32)[:, None]

    def replica(total, index):
        start = (index * TOK_DEV).astype(jnp.int32)
        token_rows = lax.dynamic_slice_in_dim(tokens, start, TOK_DEV, 0)
        upstream_rows = lax.dynamic_slice_in_dim(upstream, start, TOK_DEV, 0)
        gradient = lax.dot_general(token_rows, upstream_rows, (((0,), (0,)), ((), ())), preferred_element_type=jnp.float32)
        stored = memory[index].astype(jnp.float32)
        corrected = gradient + stored
        shards = corrected.reshape(FEAT, N_TENSOR, heads_here, HD).transpose(1, 0, 2, 3).reshape(N_TENSOR, FEAT * heads_here, HD)
        packed = jnp.take_along_axis(shards, chosen[:, :, None], axis=1)
        marks = jnp.zeros((N_TENSOR, FEAT * heads_here), jnp.float32).at[shard_ids, chosen].set(1.0)
        error = shards * (1.0 - marks[:, :, None])
        error = error.reshape(N_TENSOR, FEAT, heads_here, HD).transpose(1, 0, 2, 3).reshape(FEAT, HEADS * HD)
        updated = ((1.0 - LOWPASS) * stored + LOWPASS * error).astype(jnp.bfloat16)
        return total + packed, updated

    start_total = jnp.zeros((N_TENSOR, K, HD), jnp.float32)
    summed, memory_out = lax.scan(replica, start_total, jnp.arange(N_DP, dtype=jnp.int32))
    return summed, memory_out
```

```python
import functools

import jax
import jax.numpy as jnp
from jax import lax
from jax.experimental import pallas as pl
from jax.experimental.pallas import tpu as pltpu
from jax.sharding import PartitionSpec as P

HD = 128
LOWPASS = 0.3
NX, NZ = 4, 8
F32, BF16, I32 = jnp.float32, jnp.bfloat16, jnp.int32
MESH = pl.DeviceIdType.MESH


def dot(a, b, ca, cb):
    return lax.dot_general(a, b, (((ca,), (cb,)), ((), ())), preferred_element_type=F32)


def kernel(
    tokens, upstream, memory, lists, leader, summed, updated,
    tok, up, up_t, mem, grad_t, blocks, heads, lone, ltwo, lthree, rows_at, heads_at, index_v, index_s,
    peer_part, own_part, from_core, from_x, from_z, part,
    load_sem, index_sem, send_sem, recv_sem,
):
    features = tokens.shape[1]
    columns = upstream.shape[1]
    heads_here = columns // HD
    chosen = lists.shape[1]
    half, quarter, share = chosen // 2, chosen // 2 // NX, chosen // 2 // NX // NZ
    width = grad_t.shape[2]
    chunks = features // width

    me = lax.axis_index("dp")
    core = lax.rem(me, 2)
    z = lax.rem(me // 2, NZ)
    x = me // (2 * NZ)
    other = {"dp": me + 1 - 2 * core}

    def x_peer(step):
        return {"dp": (lax.rem(x + step, NX) * NZ + z) * 2 + core}

    def z_peer(step):
        return {"dp": (x * NZ + lax.rem(z + step, NZ)) * 2 + core}

    def remote(src, dst, at, device):
        return pltpu.make_async_remote_copy(
            src_ref=src, dst_ref=dst, send_sem=send_sem.at[at], recv_sem=recv_sem.at[at],
            device_id=device, device_id_type=MESH,
        )

    L1, L2, L3, C, X, Z, ZG, XG, CG = 0, 1, 4, 11, 15, 18, 25, 32, 35

    barrier = pltpu.get_barrier_semaphore()
    partners = [other] + [x_peer(d) for d in range(1, NX)] + [z_peer(e) for e in range(1, NZ)]
    for partner in partners:
        pl.semaphore_signal(barrier, inc=1, device_id=partner, device_id_type=MESH)

    load_up = pltpu.make_async_copy(upstream, up, load_sem.at[0])
    load_up.start()
    loads = []
    for i in range(chunks):
        at = pl.ds(i * width, width)
        load = pltpu.make_async_copy(tokens.at[:, at], tok.at[:, at], load_sem.at[1 + 2 * i])
        load.start()
        keep = pltpu.make_async_copy(memory.at[0, at], mem.at[at], load_sem.at[2 + 2 * i])
        keep.start()
        loads.append((load, keep))

    block = lists[...]
    row = lax.shift_right_logical(block * 52429, 18)
    code = (block - row * heads_here) * 4096 + row
    lone[...] = code * jnp.where(leader[0] == me, 1, 0)

    load_up.wait()
    piece = 512
    for j in range(up.shape[0] // piece):
        up_t[:, j * piece : (j + 1) * piece] = up[j * piece : (j + 1) * piece, :].T

    def finish(i):
        grad = grad_t[i % 2].T
        stored = mem[i * width : (i + 1) * width, :].astype(F32)
        for h in range(heads_here):
            cols = slice(h * HD, (h + 1) * HD)
            blocks[pl.ds(h * features + i * width, width), :] = grad[:, cols] + stored[:, cols]

    first = remote(lone, ltwo.at[0], L1, other)
    second = [remote(lone, ltwo.at[d], L2 + d - 1, x_peer(d)) for d in range(1, NX)]
    third = [remote(lone, lthree.at[e - 1], L3 + e - 1, z_peer(e)) for e in range(1, NZ)]
    index_copy = pltpu.make_async_copy(index_v, index_s, index_sem)

    for i in range(chunks):
        if i == 1:
            pl.semaphore_wait(barrier, len(partners))
            first.start()
        if i == 2:
            first.wait()
            lone[...] = lone[...] + ltwo[0]
            for copy in second:
                copy.start()
        if i == 3:
            for copy in second:
                copy.wait()
            lone[...] = lone[...] + (ltwo[1] + ltwo[2] + ltwo[3])
            for copy in third:
                copy.start()
        if i == 4:
            for copy in third:
                copy.wait()
            total = lone[...]
            for e in range(NZ - 1):
                total = total + lthree[e]
            head = lax.shift_right_logical(total, 12)
            row = total - head * 4096
            rows_at[...] = row
            heads_at[...] = head
            index_v[...] = head * features + row
            index_copy.start()
        for load in loads[i]:
            load.wait()
        grad_t[i % 2] = dot(up_t[...], tok[:, i * width : (i + 1) * width], 1, 0)
        if i > 0:
            finish(i - 1)
    finish(chunks - 1)
    index_copy.wait()

    def gather(target, slot, start):
        unroll = 16

        @pl.loop(0, quarter // unroll)
        def _(step):
            base = pl.multiple_of(step * unroll, unroll)
            for u in range(unroll):
                at = index_s[0, start + base + u]
                target[slot, pl.ds(base + u, 1), :] = blocks[pl.ds(at, 1), :]

    order = [1, 2, 3, 0]
    to_core = [remote(peer_part.at[d], from_core.at[d], C + d, other) for d in range(NX)]
    for d in order:
        gather(peer_part, d, (1 - core) * half + lax.rem(x + d, NX) * quarter)
        to_core[d].start()
    to_x = [None] + [remote(own_part.at[d], from_x.at[d - 1], X + d - 1, x_peer(d)) for d in range(1, NX)]
    for d in order:
        gather(own_part, d, core * half + lax.rem(x + d, NX) * quarter)
        to_core[d].wait_recv()
        own_part[d] = own_part[d] + from_core[d]
        if d:
            to_x[d].start()

    head_row = lax.broadcasted_iota(I32, (columns, 1), 0) // HD
    heads[...] = jnp.where(head_row == heads_at[...], 1.0, 0.0).astype(BF16)

    size = 256

    def update(i):
        at = slice(i * size, (i + 1) * size)
        feature = lax.broadcasted_iota(I32, (size, 1), 0) + i * size
        hit = jnp.where(feature == rows_at[...], 1.0, 0.0).astype(BF16)
        unsent = 1.0 - dot(hit, heads[...], 1, 1)
        for h in range(heads_here):
            cols = slice(h * HD, (h + 1) * HD)
            error = blocks[pl.ds(h * features + i * size, size), :] * unsent[:, cols]
            stored = mem[at, cols].astype(F32)
            updated[0, at, cols] = ((1.0 - LOWPASS) * stored + LOWPASS * error).astype(BF16)

    for i in range(0, 3):
        update(i)

    for d in range(1, NX):
        to_x[d].wait_recv()
    part[...] = own_part[0] + (from_x[0] + from_x[1] + from_x[2])
    to_z = [
        remote(part.at[pl.ds(lax.rem(z + e, NZ) * share, share)], from_z.at[e - 1], Z + e - 1, z_peer(e))
        for e in range(1, NZ)
    ]
    for copy in to_z:
        copy.start()
    for i in range(3, 5):
        update(i)
    for copy in to_z:
        copy.wait_recv()
    mine = part[pl.ds(pl.multiple_of(z * share, share), share), :]
    for e in range(NZ - 1):
        mine = mine + from_z[e]

    def stretch(xx, zz=None):
        if zz is None:
            return summed.at[0, pl.ds(core * half + xx * quarter, quarter)]
        return summed.at[0, pl.ds(core * half + xx * quarter + zz * share, share)]

    summed[0, pl.ds(pl.multiple_of(core * half + x * quarter + z * share, share), share), :] = mine
    out_z = [remote(stretch(x, z), stretch(x, z), ZG + e - 1, z_peer(e)) for e in range(1, NZ)]
    for copy in out_z:
        copy.start()
    for i in range(5, 7):
        update(i)
    for e in range(1, NZ):
        back = stretch(x, lax.rem(z + NZ - e, NZ))
        remote(back, back, ZG + e - 1, z_peer(e)).wait_recv()
    out_x = [remote(stretch(x), stretch(x), XG + d - 1, x_peer(d)) for d in range(1, NX)]
    for copy in out_x:
        copy.start()
    out_core = [remote(stretch(lax.rem(x + NX - d, NX)), stretch(lax.rem(x + NX - d, NX)), CG + d, other) for d in range(NX)]
    out_core[0].start()
    for i in range(7, 10):
        update(i)
    for d in range(1, NX):
        back = stretch(lax.rem(x + NX - d, NX))
        remote(back, back, XG + d - 1, x_peer(d)).wait_recv()
        out_core[d].start()
    for d in range(NX):
        back = summed.at[0, pl.ds((1 - core) * half + lax.rem(x + NX - d, NX) * quarter, quarter)]
        remote(back, back, CG + d, other).wait_recv()
    for copy in to_core + to_x[1:] + to_z + out_z + out_x + out_core:
        copy.wait_send()


def body(tokens, upstream, memory, block_lists, leader):
    count, features = tokens.shape
    columns = upstream.shape[1]
    chosen = block_lists.shape[2]
    half = chosen // 2
    quarter = half // NX
    share = quarter // NZ
    width = 512
    vmem = pl.BlockSpec(memory_space=pltpu.VMEM)
    hbm = pl.BlockSpec(memory_space=pl.ANY)
    return pl.pallas_call(
        kernel,
        out_shape=(
            jax.ShapeDtypeStruct((1, chosen, HD), F32),
            jax.ShapeDtypeStruct((1, features, columns), BF16),
        ),
        in_specs=[hbm, hbm, hbm, vmem, pl.BlockSpec(memory_space=pltpu.SMEM)],
        out_specs=(vmem, vmem),
        scratch_shapes=[
            pltpu.VMEM((count, features), BF16),
            pltpu.VMEM((count, columns), BF16),
            pltpu.VMEM((columns, count), BF16),
            pltpu.VMEM((features, columns), BF16),
            pltpu.VMEM((2, columns, width), F32),
            pltpu.VMEM((features * columns // HD, HD), F32),
            pltpu.VMEM((columns, chosen), BF16),
            pltpu.VMEM((1, chosen), I32),
            pltpu.VMEM((NX, 1, chosen), I32),
            pltpu.VMEM((NZ - 1, 1, chosen), I32),
            pltpu.VMEM((1, chosen), I32),
            pltpu.VMEM((1, chosen), I32),
            pltpu.VMEM((1, chosen), I32),
            pltpu.SMEM((1, chosen), I32),
            pltpu.VMEM((NX, quarter, HD), F32),
            pltpu.VMEM((NX, quarter, HD), F32),
            pltpu.VMEM((NX, quarter, HD), F32),
            pltpu.VMEM((NX - 1, quarter, HD), F32),
            pltpu.VMEM((NZ - 1, share, HD), F32),
            pltpu.VMEM((quarter, HD), F32),
            pltpu.SemaphoreType.DMA((1 + 2 * (features // width),)),
            pltpu.SemaphoreType.DMA,
            pltpu.SemaphoreType.DMA((39,)),
            pltpu.SemaphoreType.DMA((39,)),
        ],
        compiler_params=pltpu.CompilerParams(
            collective_id=0, has_side_effects=True, vmem_limit_bytes=48 * 2**20
        ),
        name="scalecom",
    )(tokens, upstream, memory, block_lists[0], leader)


def solution(mesh):
    placed = (
        P("dp", None),
        P("dp", "tensor"),
        P("dp", None, "tensor"),
        P("dp", "tensor", None),
        P(),
    )
    return jax.shard_map(
        body,
        mesh=mesh,
        in_specs=placed,
        out_specs=(P("tensor", None, None), P("dp", None, "tensor")),
        check_vma=False,
    )
```

```python
import functools

import jax
import jax.numpy as jnp
from jax import lax
from jax.experimental import pallas as pl
from jax.experimental.pallas import tpu as pltpu
from jax.sharding import PartitionSpec as P

HD = 128
LOWPASS = 0.3
VMEM_MIB = 40
NX, NZ = 4, 8
F32, BF16, I32 = jnp.float32, jnp.bfloat16, jnp.int32
MESH = pl.DeviceIdType.MESH


def dot(a, b, ca, cb):
    return lax.dot_general(a, b, (((ca,), (cb,)), ((), ())), preferred_element_type=F32)


def far_first():
    zs = [(NZ // 2 + (j + 1) // 2 * (1 - 2 * (j % 2))) % NZ for j in range(NZ)]
    xs = [(NX // 2 + (j + 1) // 2 * (1 - 2 * (j % 2))) % NX for j in range(NX)]
    return [(dx, dz) for dz in zs for dx in xs]


def kernel(
    tokens, upstream, memory, lists, leader, summed, updated,
    tok, up, up_t, mem, grad_t, blocks, heads, own_list, lone, peer_list, all_lists, rows_at, heads_at, index_v, index_s,
    peer_part, own_part, from_core, from_chips,
    load_sem, index_sem, send_sem, recv_sem,
):
    features = tokens.shape[1]
    columns = upstream.shape[1]
    heads_here = columns // HD
    chosen = lists.shape[1]
    half, quarter, share = chosen // 2, chosen // 2 // NX, chosen // 2 // NX // NZ
    width = grad_t.shape[2]
    chunks = features // width
    slots = NX * NZ
    chips = far_first()
    away = chips[:-1]

    me = lax.axis_index("dp")
    core = lax.rem(me, 2)
    z = lax.rem(me // 2, NZ)
    x = me // (2 * NZ)
    other = {"dp": me + 1 - 2 * core}

    def chip(dx, dz):
        return {"dp": (lax.rem(x + dx, NX) * NZ + lax.rem(z + dz, NZ)) * 2 + core}

    def remote(src, dst, at, device):
        return pltpu.make_async_remote_copy(
            src_ref=src, dst_ref=dst, send_sem=send_sem.at[at], recv_sem=recv_sem.at[at],
            device_id=device, device_id_type=MESH,
        )

    pieces = 4
    in_piece = slots // pieces
    L1, L2 = 0, 1
    C = L2 + slots - 1
    R = C + pieces
    G = R + slots - 1
    F = G + slots - 1

    barrier = pltpu.get_barrier_semaphore()
    for dx, dz in away:
        pl.semaphore_signal(barrier, inc=1, device_id=chip(dx, dz), device_id_type=MESH)
    pl.semaphore_signal(barrier, inc=1, device_id=other, device_id_type=MESH)

    load_list = pltpu.make_async_copy(lists, own_list, index_sem.at[1])
    load_list.start()
    load_up = pltpu.make_async_copy(upstream, up, load_sem.at[0])
    load_up.start()
    loads = []
    for i in range(chunks):
        at = pl.ds(i * width, width)
        load = pltpu.make_async_copy(tokens.at[:, at], tok.at[:, at], load_sem.at[1 + 2 * i])
        load.start()
        keep = pltpu.make_async_copy(memory.at[0, at], mem.at[at], load_sem.at[2 + 2 * i])
        keep.start()
        loads.append((load, keep))

    load_list.wait()
    block = own_list[...]
    row = lax.shift_right_logical(block * 52429, 18)
    code = (block - row * heads_here) * 4096 + row
    lone[...] = code * jnp.where(leader[0] == me, 1, 0)

    load_up.wait()
    piece = 512
    for j in range(up.shape[0] // piece):
        up_t[:, j * piece : (j + 1) * piece] = up[j * piece : (j + 1) * piece, :].T

    def finish(i):
        grad = grad_t[i % 2].T
        stored = mem[i * width : (i + 1) * width, :].astype(F32)
        for h in range(heads_here):
            cols = slice(h * HD, (h + 1) * HD)
            blocks[pl.ds(h * features + i * width, width), :] = grad[:, cols] + stored[:, cols]

    to_peer = remote(lone, peer_list, L1, other)
    to_all = [remote(own_list, all_lists.at[s], L2 + s, chip(dx, dz)) for s, (dx, dz) in enumerate(away)]
    index_copy = pltpu.make_async_copy(index_v, index_s, index_sem.at[0])

    for i in range(chunks):
        if i == 2:
            pl.semaphore_wait(barrier, slots)
            to_peer.start()
            to_peer.wait()
            own_list[...] = lone[...] + peer_list[...]
            for copy in to_all:
                copy.start()
        for load in loads[i]:
            load.wait()
        grad_t[i % 2] = dot(up_t[...], tok[:, i * width : (i + 1) * width], 1, 0)
        if i > 0:
            finish(i - 1)
    finish(chunks - 1)

    for copy in to_all:
        copy.wait_recv()
    total = own_list[...]
    for s in range(slots - 1):
        total = total + all_lists[s]
    head = lax.shift_right_logical(total, 12)
    row = total - head * 4096
    rows_at[...] = row
    heads_at[...] = head
    index_v[...] = head * features + row
    index_copy.start()
    index_copy.wait()

    def bent(j, n):
        return lax.rem(n // 2 + (j + 1) // 2 * (1 - 2 * lax.rem(j, 2)), n)

    def gather(target, piece, first_row):
        @pl.loop(0, in_piece)
        def _(step):
            slot = piece * in_piece + step
            to_x = lax.rem(x + bent(lax.rem(slot, NX), NX), NX)
            to_z = lax.rem(z + bent(slot // NX, NZ), NZ)
            start = first_row + (to_x * NZ + to_z) * share
            base = pl.multiple_of(slot * share, share)
            for u in range(share):
                at = index_s[0, start + u]
                target[pl.ds(base + u, 1), :] = blocks[pl.ds(at, 1), :]

    to_core = []
    for p in range(pieces):
        gather(peer_part, p, (1 - core) * half)
        rows = pl.ds(p * quarter, quarter)
        copy = remote(peer_part.at[rows], from_core.at[rows], C + p, other)
        copy.start()
        to_core.append(copy)
    to_chips = []
    for p in range(pieces):
        gather(own_part, p, core * half)
        to_core[p].wait_recv()
        rows = slice(p * quarter, (p + 1) * quarter)
        own_part[rows, :] = own_part[rows, :] + from_core[rows, :]
        for s in range(p * in_piece, min((p + 1) * in_piece, slots - 1)):
            copy = remote(own_part.at[pl.ds(s * share, share)], from_chips.at[s], R + s, chip(*chips[s]))
            copy.start()
            to_chips.append(copy)

    head_row = lax.broadcasted_iota(I32, (columns, 1), 0) // HD
    heads[...] = jnp.where(head_row == heads_at[...], 1.0, 0.0).astype(BF16)

    size = 256

    def update(i):
        at = slice(i * size, (i + 1) * size)
        feature = lax.broadcasted_iota(I32, (size, 1), 0) + i * size
        hit = jnp.where(feature == rows_at[...], 1.0, 0.0).astype(BF16)
        unsent = 1.0 - dot(hit, heads[...], 1, 1)
        for h in range(heads_here):
            cols = slice(h * HD, (h + 1) * HD)
            error = blocks[pl.ds(h * features + i * size, size), :] * unsent[:, cols]
            stored = mem[at, cols].astype(F32)
            updated[0, at, cols] = ((1.0 - LOWPASS) * stored + LOWPASS * error).astype(BF16)

    for i in range(0, 8):
        update(i)

    for copy in to_chips:
        copy.wait_recv()
    mine = own_part[(slots - 1) * share : slots * share, :]
    for s in range(slots - 1):
        mine = mine + from_chips[s]

    def share_of(xx, zz):
        return summed.at[0, pl.ds(core * half + xx * quarter + zz * share, share)]

    def quarter_of(cc, xx):
        return summed.at[0, pl.ds(cc * half + xx * quarter, quarter)]

    summed[0, pl.ds(pl.multiple_of(core * half + x * quarter + z * share, share), share), :] = mine
    out = [remote(share_of(x, z), share_of(x, z), G + s, chip(dx, dz)) for s, (dx, dz) in enumerate(away)]
    for copy in out:
        copy.start()
    for i in range(8, features // size):
        update(i)
    to_other = []
    for dx in (0, 1, NX - 1, 2):
        from_x = lax.rem(x + NX - dx, NX)
        for s, (sx, sz) in enumerate(away):
            if sx == dx:
                back = share_of(from_x, lax.rem(z + NZ - sz, NZ))
                remote(back, back, G + s, chip(sx, sz)).wait_recv()
        copy = remote(quarter_of(core, from_x), quarter_of(core, from_x), F + dx, other)
        copy.start()
        to_other.append(copy)
    for dx in (0, 1, NX - 1, 2):
        back = quarter_of(1 - core, lax.rem(x + NX - dx, NX))
        remote(back, back, F + dx, other).wait_recv()
    for copy in to_all + to_core + to_chips + out + to_other:
        copy.wait_send()


def body(tokens, upstream, memory, block_lists, leader):
    count, features = tokens.shape
    columns = upstream.shape[1]
    chosen = block_lists.shape[2]
    half = chosen // 2
    quarter = half // NX
    share = quarter // NZ
    width = 512
    hbm = pl.BlockSpec(memory_space=pltpu.HBM)
    vmem = pl.BlockSpec(memory_space=pltpu.VMEM)
    copies = 3 * (NX * NZ - 1) + 9
    summed, updated = pl.pallas_call(
        kernel,
        out_shape=(
            pltpu.VMEM((1, chosen, HD), F32),
            pltpu.VMEM((1, features, columns), BF16),
        ),
        in_specs=[hbm, hbm, hbm, hbm, pl.BlockSpec(memory_space=pltpu.SMEM)],
        out_specs=(vmem, vmem),
        scratch_shapes=[
            pltpu.VMEM((count, features), BF16),
            pltpu.VMEM((count, columns), BF16),
            pltpu.VMEM((columns, count), BF16),
            pltpu.VMEM((features, columns), BF16),
            pltpu.VMEM((2, columns, width), F32),
            pltpu.VMEM((features * columns // HD, HD), F32),
            pltpu.VMEM((columns, chosen), BF16),
            pltpu.VMEM((1, chosen), I32),
            pltpu.VMEM((1, chosen), I32),
            pltpu.VMEM((1, chosen), I32),
            pltpu.VMEM((NX * NZ - 1, 1, chosen), I32),
            pltpu.VMEM((1, chosen), I32),
            pltpu.VMEM((1, chosen), I32),
            pltpu.VMEM((1, chosen), I32),
            pltpu.SMEM((1, chosen), I32),
            pltpu.VMEM((half, HD), F32),
            pltpu.VMEM((half, HD), F32),
            pltpu.VMEM((half, HD), F32),
            pltpu.VMEM((NX * NZ - 1, share, HD), F32),
            pltpu.SemaphoreType.DMA((1 + 2 * (features // width),)),
            pltpu.SemaphoreType.DMA((2,)),
            pltpu.SemaphoreType.DMA((copies,)),
            pltpu.SemaphoreType.DMA((copies,)),
        ],
        compiler_params=pltpu.CompilerParams(
            collective_id=0, has_side_effects=True, vmem_limit_bytes=VMEM_MIB * 2**20
        ),
        name="scalecom",
    )(*(pltpu.with_memory_space_constraint(a, pltpu.HBM) for a in (tokens, upstream, memory, block_lists[0])), leader)
    return summed, updated


def solution(mesh):
    placed = (
        P("dp", None),
        P("dp", "tensor"),
        P("dp", None, "tensor"),
        P("dp", "tensor", None),
        P(),
    )
    return jax.shard_map(
        body,
        mesh=mesh,
        in_specs=placed,
        out_specs=(P("tensor", None, None), P("dp", None, "tensor")),
        check_vma=False,
    )
```

```python
import functools

import jax
import jax.numpy as jnp
from jax import lax
from jax.experimental import pallas as pl
from jax.experimental.pallas import tpu as pltpu
from jax.sharding import PartitionSpec as P

HD = 128
LOWPASS = 0.3
VMEM_MIB = 40
SIZES = (512, 512, 512, 512, 512)
LIST_AT = 1
ORDER = (0, 1, 4, 2, 5, 3, 6, 7)
UPDATES = (8, 2)
STAGGER = ()
NX, NZ = 4, 8
F32, BF16, I32 = jnp.float32, jnp.bfloat16, jnp.int32
MESH = pl.DeviceIdType.MESH


def dot(a, b, ca, cb):
    return lax.dot_general(a, b, (((ca,), (cb,)), ((), ())), preferred_element_type=F32)


def far_first():
    zs = [(NZ // 2 + (j + 1) // 2 * (1 - 2 * (j % 2))) % NZ for j in range(NZ)]
    xs = [(NX // 2 + (j + 1) // 2 * (1 - 2 * (j % 2))) % NX for j in range(NX)]
    return [(dx, dz) for dz in zs for dx in xs]


def kernel(
    tokens, upstream, memory, lists, leader, summed, updated,
    tok, up, mem, blocks, heads, own_list, lone, peer_list, all_lists, rows_at, heads_at, index_v, index_s,
    peer_part, own_part, from_core, from_chips,
    load_sem, index_sem, send_sem, recv_sem,
):
    features = tokens.shape[1]
    columns = upstream.shape[1]
    heads_here = columns // HD
    chosen = lists.shape[1]
    half, quarter, share = chosen // 2, chosen // 2 // NX, chosen // 2 // NX // NZ
    offsets = [sum(SIZES[:i]) for i in range(len(SIZES))]
    chunks = len(SIZES)
    slots = NX * NZ
    chips = far_first()
    away = chips[:-1]

    me = lax.axis_index("dp")
    core = lax.rem(me, 2)
    z = lax.rem(me // 2, NZ)
    x = me // (2 * NZ)
    other = {"dp": me + 1 - 2 * core}

    def chip(dx, dz):
        return {"dp": (lax.rem(x + dx, NX) * NZ + lax.rem(z + dz, NZ)) * 2 + core}

    def remote(src, dst, at, device):
        return pltpu.make_async_remote_copy(
            src_ref=src, dst_ref=dst, send_sem=send_sem.at[at], recv_sem=recv_sem.at[at],
            device_id=device, device_id_type=MESH,
        )

    pieces = 4
    in_piece = slots // pieces
    L1, L2 = 0, 1
    C = L2 + slots - 1
    R = C + pieces
    G = R + slots - 1
    F = G + slots - 1

    barrier = pltpu.get_barrier_semaphore()
    for dx, dz in away:
        pl.semaphore_signal(barrier, inc=1, device_id=chip(dx, dz), device_id_type=MESH)
    pl.semaphore_signal(barrier, inc=1, device_id=other, device_id_type=MESH)

    load_list = pltpu.make_async_copy(lists, own_list, index_sem.at[1])
    load_list.start()
    load_up = pltpu.make_async_copy(upstream, up, load_sem.at[0])
    load_up.start()
    loads, keeps = [], []
    for i in range(chunks):
        at = pl.ds(offsets[i], SIZES[i])
        loads.append(pltpu.make_async_copy(tokens.at[:, at], tok.at[:, at], load_sem.at[1 + 2 * i]))
        keeps.append(pltpu.make_async_copy(memory.at[0, at], mem.at[at], load_sem.at[2 + 2 * i]))

    loads[0].start()
    keeps[0].start()

    load_list.wait()
    block = own_list[...]
    row = lax.shift_right_logical(block * 52429, 18)
    code = (block - row * heads_here) * 4096 + row
    lone[...] = code * jnp.where(leader[0] == me, 1, 0)

    to_peer = remote(lone, peer_list, L1, other)
    to_all = [remote(own_list, all_lists.at[s], L2 + s, chip(dx, dz)) for s, (dx, dz) in enumerate(away)]
    index_copy = pltpu.make_async_copy(index_v, index_s, index_sem.at[0])

    for i in range(chunks):
        if i == LIST_AT:
            pl.semaphore_wait(barrier, slots)
            to_peer.start()
            to_peer.wait()
            own_list[...] = lone[...] + peer_list[...]
            for copy in to_all:
                copy.start()
        if i == 0:
            load_up.wait()
        loads[i].wait()
        keeps[i].wait()
        if i + 1 < chunks:
            loads[i + 1].start()
            keeps[i + 1].start()
        at = slice(offsets[i], offsets[i] + SIZES[i])
        grad = dot(tok[:, at], up[...], 0, 0)
        for h in range(heads_here):
            cols = slice(h * HD, (h + 1) * HD)
            blocks[pl.ds(h * features + offsets[i], SIZES[i]), :] = grad[:, cols] + mem[at, cols].astype(F32)

    for copy in to_all:
        copy.wait_recv()
    total = own_list[...]
    for s in range(slots - 1):
        total = total + all_lists[s]
    head = lax.shift_right_logical(total, 12)
    row = total - head * 4096
    rows_at[...] = row
    heads_at[...] = head
    index_v[...] = head * features + row
    index_copy.start()
    index_copy.wait()

    def bent(j, n):
        return (n // 2 + ((j + 1) >> 1) * (1 - 2 * (j & 1))) & (n - 1)

    def gather(target, piece, first_row):
        @pl.loop(0, in_piece)
        def _(step):
            slot = piece * in_piece + step
            to_x = (x + bent(slot & (NX - 1), NX)) & (NX - 1)
            to_z = (z + bent(slot >> 2, NZ)) & (NZ - 1)
            start = first_row + (to_x * NZ + to_z) * share
            base = pl.multiple_of(slot * share, share)
            found = [blocks[pl.ds(index_s[0, start + u], 1), :] for u in range(share)]
            for u in range(share):
                target[pl.ds(base + u, 1), :] = found[u]

    to_core = [
        remote(peer_part.at[pl.ds(p * quarter, quarter)], from_core.at[pl.ds(p * quarter, quarter)], C + p, other)
        for p in range(pieces)
    ]
    to_chips = []
    for turn in ORDER:
        p = turn % pieces
        if turn < pieces:
            gather(peer_part, p, (1 - core) * half)
            to_core[p].start()
            continue
        gather(own_part, p, core * half)
        to_core[p].wait_recv()
        rows = slice(p * quarter, (p + 1) * quarter)
        own_part[rows, :] = own_part[rows, :] + from_core[rows, :]
        for s in range(p * in_piece, min((p + 1) * in_piece, slots - 1)):
            copy = remote(own_part.at[pl.ds(s * share, share)], from_chips.at[s], R + s, chip(*chips[s]))
            copy.start()
            to_chips.append(copy)

    head_row = lax.broadcasted_iota(I32, (columns, 1), 0) // HD
    heads[...] = jnp.where(head_row == heads_at[...], 1.0, 0.0).astype(BF16)

    size = 256

    def update(i):
        at = slice(i * size, (i + 1) * size)
        feature = lax.broadcasted_iota(I32, (size, 1), 0) + i * size
        hit = jnp.where(feature == rows_at[...], 1.0, 0.0).astype(BF16)
        unsent = 1.0 - dot(hit, heads[...], 1, 1)
        for h in range(heads_here):
            cols = slice(h * HD, (h + 1) * HD)
            error = blocks[pl.ds(h * features + i * size, size), :] * unsent[:, cols]
            stored = mem[at, cols].astype(F32)
            updated[0, at, cols] = ((1.0 - LOWPASS) * stored + LOWPASS * error).astype(BF16)

    for i in range(0, UPDATES[0]):
        update(i)

    for copy in to_chips:
        copy.wait_recv()
    mine = own_part[(slots - 1) * share : slots * share, :]
    for s in range(slots - 1):
        mine = mine + from_chips[s]

    def share_of(xx, zz):
        return summed.at[0, pl.ds(core * half + xx * quarter + zz * share, share)]

    def quarter_of(cc, xx):
        return summed.at[0, pl.ds(cc * half + xx * quarter, quarter)]

    summed[0, pl.ds(pl.multiple_of(core * half + x * quarter + z * share, share), share), :] = mine
    out = [remote(share_of(x, z), share_of(x, z), G + s, chip(dx, dz)) for s, (dx, dz) in enumerate(away)]
    done = UPDATES[0]
    for s, copy in enumerate(out):
        copy.start()
        if s in STAGGER:
            update(done)
            done += 1
    for i in range(done, features // size):
        update(i)
    to_other = []
    for dx in (0, 1, NX - 1, 2):
        from_x = lax.rem(x + NX - dx, NX)
        for s, (sx, sz) in enumerate(away):
            if sx == dx:
                back = share_of(from_x, lax.rem(z + NZ - sz, NZ))
                remote(back, back, G + s, chip(sx, sz)).wait_recv()
        copy = remote(quarter_of(core, from_x), quarter_of(core, from_x), F + dx, other)
        copy.start()
        to_other.append(copy)
    for dx in (0, 1, NX - 1, 2):
        back = quarter_of(1 - core, lax.rem(x + NX - dx, NX))
        remote(back, back, F + dx, other).wait_recv()
    for copy in to_all + to_core + to_chips + out + to_other:
        copy.wait_send()


def flush(summed, updated, summed_out, updated_out, sem):
    copies = [
        pltpu.make_async_copy(updated, updated_out, sem.at[0]),
        pltpu.make_async_copy(summed, summed_out, sem.at[1]),
    ]
    for copy in copies:
        copy.start()
    for copy in copies:
        copy.wait()


def body(tokens, upstream, memory, block_lists, leader):
    count, features = tokens.shape
    columns = upstream.shape[1]
    chosen = block_lists.shape[2]
    half = chosen // 2
    quarter = half // NX
    share = quarter // NZ
    hbm = pl.BlockSpec(memory_space=pltpu.HBM)
    vmem = pl.BlockSpec(memory_space=pltpu.VMEM)
    copies = 3 * (NX * NZ - 1) + 9
    summed, updated = pl.pallas_call(
        kernel,
        out_shape=(
            pltpu.VMEM((1, chosen, HD), F32),
            pltpu.VMEM((1, features, columns), BF16),
        ),
        in_specs=[hbm, hbm, hbm, hbm, pl.BlockSpec(memory_space=pltpu.SMEM)],
        out_specs=(vmem, vmem),
        scratch_shapes=[
            pltpu.VMEM((count, features), BF16),
            pltpu.VMEM((count, columns), BF16),
            pltpu.VMEM((features, columns), BF16),
            pltpu.VMEM((features * columns // HD, HD), F32),
            pltpu.VMEM((columns, chosen), BF16),
            pltpu.VMEM((1, chosen), I32),
            pltpu.VMEM((1, chosen), I32),
            pltpu.VMEM((1, chosen), I32),
            pltpu.VMEM((NX * NZ - 1, 1, chosen), I32),
            pltpu.VMEM((1, chosen), I32),
            pltpu.VMEM((1, chosen), I32),
            pltpu.VMEM((1, chosen), I32),
            pltpu.SMEM((1, chosen), I32),
            pltpu.VMEM((half, HD), F32),
            pltpu.VMEM((half, HD), F32),
            pltpu.VMEM((half, HD), F32),
            pltpu.VMEM((NX * NZ - 1, share, HD), F32),
            pltpu.SemaphoreType.DMA((1 + 2 * len(SIZES),)),
            pltpu.SemaphoreType.DMA((2,)),
            pltpu.SemaphoreType.DMA((copies,)),
            pltpu.SemaphoreType.DMA((copies,)),
        ],
        compiler_params=pltpu.CompilerParams(
            collective_id=0, has_side_effects=True, vmem_limit_bytes=VMEM_MIB * 2**20
        ),
        name="scalecom",
    )(*(pltpu.with_memory_space_constraint(a, pltpu.HBM) for a in (tokens, upstream, memory, block_lists[0])), leader)
    return pl.pallas_call(
        flush,
        out_shape=(
            jax.ShapeDtypeStruct(summed.shape, F32),
            jax.ShapeDtypeStruct(updated.shape, BF16),
        ),
        in_specs=[vmem, vmem],
        out_specs=(hbm, hbm),
        scratch_shapes=[pltpu.SemaphoreType.DMA((2,))],
        name="flush",
    )(summed, updated)


def solution(mesh):
    placed = (
        P("dp", None),
        P("dp", "tensor"),
        P("dp", None, "tensor"),
        P("dp", "tensor", None),
        P(),
    )
    return jax.shard_map(
        body,
        mesh=mesh,
        in_specs=placed,
        out_specs=(P("tensor", None, None), P("dp", None, "tensor")),
        check_vma=False,
    )
```

```python
import functools

import jax
import jax.numpy as jnp
from jax import lax
from jax.experimental import pallas as pl
from jax.experimental.pallas import tpu as pltpu
from jax.sharding import PartitionSpec as P

HD = 128
LOWPASS = 0.3
VMEM_MIB = 40
SIZES = (512, 512, 512, 512, 512)
LIST_AT = 1
ORDER = (0, 1, 4, 2, 5, 3, 6, 7)
UPDATES = (8, 2)
STAGGER = ()
NX, NZ = 4, 8
F32, BF16, I32 = jnp.float32, jnp.bfloat16, jnp.int32
MESH = pl.DeviceIdType.MESH


def dot(a, b, ca, cb):
    return lax.dot_general(a, b, (((ca,), (cb,)), ((), ())), preferred_element_type=F32)


def far_first():
    zs = [(NZ // 2 + (j + 1) // 2 * (1 - 2 * (j % 2))) % NZ for j in range(NZ)]
    xs = [(NX // 2 + (j + 1) // 2 * (1 - 2 * (j % 2))) % NX for j in range(NX)]
    return [(dx, dz) for dz in zs for dx in xs]


def kernel(
    tokens, upstream, memory, lists, leader, summed, updated,
    tok, up, mem, blocks, heads, own_list, lone, peer_list, all_lists, rows_at, heads_at, index_v, index_s,
    peer_part, own_part, from_core, from_chips,
    load_sem, index_sem, send_sem, recv_sem,
):
    features = tokens.shape[1]
    columns = upstream.shape[1]
    heads_here = columns // HD
    chosen = lists.shape[1]
    half, quarter, share = chosen // 2, chosen // 2 // NX, chosen // 2 // NX // NZ
    offsets = [sum(SIZES[:i]) for i in range(len(SIZES))]
    chunks = len(SIZES)
    slots = NX * NZ
    chips = far_first()
    away = chips[:-1]

    me = lax.axis_index("dp")
    core = lax.rem(me, 2)
    z = lax.rem(me // 2, NZ)
    x = me // (2 * NZ)
    other = {"dp": me + 1 - 2 * core}

    def chip(dx, dz):
        return {"dp": (lax.rem(x + dx, NX) * NZ + lax.rem(z + dz, NZ)) * 2 + core}

    def remote(src, dst, at, device):
        return pltpu.make_async_remote_copy(
            src_ref=src, dst_ref=dst, send_sem=send_sem.at[at], recv_sem=recv_sem.at[at],
            device_id=device, device_id_type=MESH,
        )

    pieces = 4
    in_piece = slots // pieces
    L1, L2 = 0, 1
    C = L2 + slots - 1
    R = C + pieces
    G = R + slots - 1
    F = G + slots - 1

    barrier = pltpu.get_barrier_semaphore()
    for dx, dz in away:
        pl.semaphore_signal(barrier, inc=1, device_id=chip(dx, dz), device_id_type=MESH)
    pl.semaphore_signal(barrier, inc=1, device_id=other, device_id_type=MESH)

    load_list = pltpu.make_async_copy(lists, own_list, index_sem.at[1])
    load_list.start()
    load_up = pltpu.make_async_copy(upstream, up, load_sem.at[0])
    load_up.start()
    loads, keeps = [], []
    for i in range(chunks):
        at = pl.ds(offsets[i], SIZES[i])
        loads.append(pltpu.make_async_copy(tokens.at[:, at], tok.at[:, at], load_sem.at[1 + 2 * i]))
        keeps.append(pltpu.make_async_copy(memory.at[0, at], mem.at[at], load_sem.at[2 + 2 * i]))

    loads[0].start()
    keeps[0].start()

    load_list.wait()
    block = own_list[...]
    row = lax.shift_right_logical(block * 52429, 18)
    code = (block - row * heads_here) * 4096 + row
    lone[...] = code * jnp.where(leader[0] == me, 1, 0)

    to_peer = remote(lone, peer_list, L1, other)
    to_all = [remote(own_list, all_lists.at[s], L2 + s, chip(dx, dz)) for s, (dx, dz) in enumerate(away)]
    index_copy = pltpu.make_async_copy(index_v, index_s, index_sem.at[0])

    for i in range(chunks):
        if i == LIST_AT:
            pl.semaphore_wait(barrier, slots)
            to_peer.start()
            to_peer.wait()
            own_list[...] = lone[...] + peer_list[...]
            for copy in to_all:
                copy.start()
        if i == 0:
            load_up.wait()
        loads[i].wait()
        keeps[i].wait()
        if i + 1 < chunks:
            loads[i + 1].start()
            keeps[i + 1].start()
        at = slice(offsets[i], offsets[i] + SIZES[i])
        grad = dot(tok[:, at], up[...], 0, 0)
        for h in range(heads_here):
            cols = slice(h * HD, (h + 1) * HD)
            blocks[pl.ds(h * features + offsets[i], SIZES[i]), :] = grad[:, cols] + mem[at, cols].astype(F32)

    for copy in to_all:
        copy.wait_recv()
    total = own_list[...]
    for s in range(slots - 1):
        total = total + all_lists[s]
    head = lax.shift_right_logical(total, 12)
    row = total - head * 4096
    rows_at[...] = row
    heads_at[...] = head
    index_v[...] = head * features + row
    index_copy.start()
    index_copy.wait()

    def bent(j, n):
        return (n // 2 + ((j + 1) >> 1) * (1 - 2 * (j & 1))) & (n - 1)

    def gather(target, piece, first_row):
        @pl.loop(0, in_piece)
        def _(step):
            slot = piece * in_piece + step
            to_x = (x + bent(slot & (NX - 1), NX)) & (NX - 1)
            to_z = (z + bent(slot >> 2, NZ)) & (NZ - 1)
            start = first_row + (to_x * NZ + to_z) * share
            base = pl.multiple_of(slot * share, share)
            found = [blocks[pl.ds(index_s[0, start + u], 1), :] for u in range(share)]
            for u in range(share):
                target[pl.ds(base + u, 1), :] = found[u]

    to_core = [
        remote(peer_part.at[pl.ds(p * quarter, quarter)], from_core.at[pl.ds(p * quarter, quarter)], C + p, other)
        for p in range(pieces)
    ]
    to_chips = []
    for turn in ORDER:
        p = turn % pieces
        if turn < pieces:
            gather(peer_part, p, (1 - core) * half)
            to_core[p].start()
            continue
        gather(own_part, p, core * half)
        to_core[p].wait_recv()
        rows = slice(p * quarter, (p + 1) * quarter)
        own_part[rows, :] = own_part[rows, :] + from_core[rows, :]
        for s in range(p * in_piece, min((p + 1) * in_piece, slots - 1)):
            copy = remote(own_part.at[pl.ds(s * share, share)], from_chips.at[s], R + s, chip(*chips[s]))
            copy.start()
            to_chips.append(copy)

    head_row = lax.broadcasted_iota(I32, (columns, 1), 0) // HD
    heads[...] = jnp.where(head_row == heads_at[...], 1.0, 0.0).astype(BF16)

    size = 256

    def update(i):
        at = slice(i * size, (i + 1) * size)
        feature = lax.broadcasted_iota(I32, (size, 1), 0) + i * size
        hit = jnp.where(feature == rows_at[...], 1.0, 0.0).astype(BF16)
        unsent = 1.0 - dot(hit, heads[...], 1, 1)
        for h in range(heads_here):
            cols = slice(h * HD, (h + 1) * HD)
            error = blocks[pl.ds(h * features + i * size, size), :] * unsent[:, cols]
            stored = mem[at, cols].astype(F32)
            updated[0, at, cols] = ((1.0 - LOWPASS) * stored + LOWPASS * error).astype(BF16)

    for i in range(0, UPDATES[0]):
        update(i)

    for copy in to_chips:
        copy.wait_recv()
    mine = own_part[(slots - 1) * share : slots * share, :]
    for s in range(slots - 1):
        mine = mine + from_chips[s]

    def share_of(xx, zz):
        return summed.at[0, pl.ds(core * half + xx * quarter + zz * share, share)]

    def quarter_of(cc, xx):
        return summed.at[0, pl.ds(cc * half + xx * quarter, quarter)]

    summed[0, pl.ds(pl.multiple_of(core * half + x * quarter + z * share, share), share), :] = mine
    out = [remote(share_of(x, z), share_of(x, z), G + s, chip(dx, dz)) for s, (dx, dz) in enumerate(away)]
    done = UPDATES[0]
    for s, copy in enumerate(out):
        copy.start()
        if s in STAGGER:
            update(done)
            done += 1
    for i in range(done, features // size):
        update(i)
    to_other = []
    for dx in (0, 1, NX - 1, 2):
        from_x = lax.rem(x + NX - dx, NX)
        for s, (sx, sz) in enumerate(away):
            if sx == dx:
                back = share_of(from_x, lax.rem(z + NZ - sz, NZ))
                remote(back, back, G + s, chip(sx, sz)).wait_recv()
        copy = remote(quarter_of(core, from_x), quarter_of(core, from_x), F + dx, other)
        copy.start()
        to_other.append(copy)
    for dx in (0, 1, NX - 1, 2):
        back = quarter_of(1 - core, lax.rem(x + NX - dx, NX))
        remote(back, back, F + dx, other).wait_recv()
    for copy in to_all + to_core + to_chips + out + to_other:
        copy.wait_send()


def flush(summed, updated, summed_out, updated_out, sem):
    copies = [
        pltpu.make_async_copy(updated, updated_out, sem.at[0]),
        pltpu.make_async_copy(summed, summed_out, sem.at[1]),
    ]
    for copy in copies:
        copy.start()
    for copy in copies:
        copy.wait()


def body(tokens, upstream, memory, block_lists, leader):
    count, features = tokens.shape
    columns = upstream.shape[1]
    chosen = block_lists.shape[2]
    half = chosen // 2
    quarter = half // NX
    share = quarter // NZ
    hbm = pl.BlockSpec(memory_space=pltpu.HBM)
    vmem = pl.BlockSpec(memory_space=pltpu.VMEM)
    copies = 3 * (NX * NZ - 1) + 9
    summed, updated = pl.pallas_call(
        kernel,
        out_shape=(
            pltpu.VMEM((1, chosen, HD), F32),
            pltpu.VMEM((1, features, columns), BF16),
        ),
        in_specs=[hbm, hbm, hbm, hbm, pl.BlockSpec(memory_space=pltpu.SMEM)],
        out_specs=(vmem, vmem),
        scratch_shapes=[
            pltpu.VMEM((count, features), BF16),
            pltpu.VMEM((count, columns), BF16),
            pltpu.VMEM((features, columns), BF16),
            pltpu.VMEM((features * columns // HD, HD), F32),
            pltpu.VMEM((columns, chosen), BF16),
            pltpu.VMEM((1, chosen), I32),
            pltpu.VMEM((1, chosen), I32),
            pltpu.VMEM((1, chosen), I32),
            pltpu.VMEM((NX * NZ - 1, 1, chosen), I32),
            pltpu.VMEM((1, chosen), I32),
            pltpu.VMEM((1, chosen), I32),
            pltpu.VMEM((1, chosen), I32),
            pltpu.SMEM((1, chosen), I32),
            pltpu.VMEM((half, HD), F32),
            pltpu.VMEM((half, HD), F32),
            pltpu.VMEM((half, HD), F32),
            pltpu.VMEM((NX * NZ - 1, share, HD), F32),
            pltpu.SemaphoreType.DMA((1 + 2 * len(SIZES),)),
            pltpu.SemaphoreType.DMA((2,)),
            pltpu.SemaphoreType.DMA((copies,)),
            pltpu.SemaphoreType.DMA((copies,)),
        ],
        compiler_params=pltpu.CompilerParams(
            collective_id=0, has_side_effects=True, vmem_limit_bytes=VMEM_MIB * 2**20
        ),
        name="scalecom",
    )(*(pltpu.with_memory_space_constraint(a, pltpu.HBM) for a in (tokens, upstream, memory, block_lists[0])), leader)
    return pl.pallas_call(
        flush,
        out_shape=(
            jax.ShapeDtypeStruct(summed.shape, F32),
            jax.ShapeDtypeStruct(updated.shape, BF16),
        ),
        in_specs=[vmem, vmem],
        out_specs=(hbm, hbm),
        scratch_shapes=[pltpu.SemaphoreType.DMA((2,))],
        compiler_params=pltpu.CompilerParams(vmem_limit_bytes=2**20),
        name="flush",
    )(*(pltpu.with_memory_space_constraint(a, pltpu.VMEM) for a in (summed, updated)))


def solution(mesh):
    placed = (
        P("dp", None),
        P("dp", "tensor"),
        P("dp", None, "tensor"),
        P("dp", "tensor", None),
        P(),
    )
    return jax.shard_map(
        body,
        mesh=mesh,
        in_specs=placed,
        out_specs=(P("tensor", None, None), P("dp", None, "tensor")),
        check_vma=False,
    )
```

```python
import functools

import jax
import jax.numpy as jnp
from jax import lax
from jax.experimental import pallas as pl
from jax.experimental.pallas import tpu as pltpu
from jax.sharding import PartitionSpec as P

HD = 128
LOWPASS = 0.3
VMEM_MIB = 40
SIZES = (512, 512, 512, 512, 512)
LIST_AT = 1
ORDER = (0, 1, 4, 2, 5, 3, 6, 7)
UPDATES = (6, 4)
STAGGER = ()
NX, NZ = 4, 8
F32, BF16, I32 = jnp.float32, jnp.bfloat16, jnp.int32
MESH = pl.DeviceIdType.MESH


def dot(a, b, ca, cb):
    return lax.dot_general(a, b, (((ca,), (cb,)), ((), ())), preferred_element_type=F32)


def far_first():
    zs = [(NZ // 2 + (j + 1) // 2 * (1 - 2 * (j % 2))) % NZ for j in range(NZ)]
    xs = [(NX // 2 + (j + 1) // 2 * (1 - 2 * (j % 2))) % NX for j in range(NX)]
    return [(dx, dz) for dz in zs for dx in xs]


def kernel(
    tokens, upstream, memory, lists, leader, summed, updated,
    tok, up, mem, blocks, heads, own_list, lone, peer_list, all_lists, rows_at, heads_at, index_v, index_s,
    peer_part, own_part, from_core, from_chips,
    load_sem, index_sem, send_sem, recv_sem,
):
    features = tokens.shape[1]
    columns = upstream.shape[1]
    heads_here = columns // HD
    chosen = lists.shape[1]
    half, quarter, share = chosen // 2, chosen // 2 // NX, chosen // 2 // NX // NZ
    offsets = [sum(SIZES[:i]) for i in range(len(SIZES))]
    chunks = len(SIZES)
    slots = NX * NZ
    chips = far_first()
    away = chips[:-1]

    me = lax.axis_index("dp")
    core = lax.rem(me, 2)
    z = lax.rem(me // 2, NZ)
    x = me // (2 * NZ)
    other = {"dp": me + 1 - 2 * core}

    def chip(dx, dz):
        return {"dp": (lax.rem(x + dx, NX) * NZ + lax.rem(z + dz, NZ)) * 2 + core}

    def remote(src, dst, at, device):
        return pltpu.make_async_remote_copy(
            src_ref=src, dst_ref=dst, send_sem=send_sem.at[at], recv_sem=recv_sem.at[at],
            device_id=device, device_id_type=MESH,
        )

    pieces = 4
    in_piece = slots // pieces
    L1, L2 = 0, 1
    C = L2 + slots - 1
    R = C + pieces
    G = R + slots - 1
    F = G + slots - 1

    barrier = pltpu.get_barrier_semaphore()
    load_list = pltpu.make_async_copy(lists, own_list, index_sem.at[1])
    load_list.start()
    load_up = pltpu.make_async_copy(upstream, up, load_sem.at[0])
    load_up.start()
    loads, keeps = [], []
    for i in range(chunks):
        at = pl.ds(offsets[i], SIZES[i])
        loads.append(pltpu.make_async_copy(tokens.at[:, at], tok.at[:, at], load_sem.at[1 + 2 * i]))
        keeps.append(pltpu.make_async_copy(memory.at[0, at], mem.at[at], load_sem.at[2 + 2 * i]))

    loads[0].start()
    keeps[0].start()
    for dx, dz in away:
        pl.semaphore_signal(barrier, inc=1, device_id=chip(dx, dz), device_id_type=MESH)
    pl.semaphore_signal(barrier, inc=1, device_id=other, device_id_type=MESH)

    load_list.wait()
    block = own_list[...]
    row = lax.shift_right_logical(block * 52429, 18)
    code = (block - row * heads_here) * 4096 + row
    lone[...] = code * jnp.where(leader[0] == me, 1, 0)

    to_peer = remote(lone, peer_list, L1, other)
    to_all = [remote(own_list, all_lists.at[s], L2 + s, chip(dx, dz)) for s, (dx, dz) in enumerate(away)]
    index_copy = pltpu.make_async_copy(index_v, index_s, index_sem.at[0])

    for i in range(chunks):
        if i == LIST_AT:
            pl.semaphore_wait(barrier, slots)
            to_peer.start()
            to_peer.wait()
            own_list[...] = lone[...] + peer_list[...]
            for copy in to_all:
                copy.start()
        if i == 0:
            load_up.wait()
        loads[i].wait()
        keeps[i].wait()
        if i + 1 < chunks:
            loads[i + 1].start()
            keeps[i + 1].start()
        at = slice(offsets[i], offsets[i] + SIZES[i])
        grad = dot(tok[:, at], up[...], 0, 0)
        for h in range(heads_here):
            cols = slice(h * HD, (h + 1) * HD)
            blocks[pl.ds(h * features + offsets[i], SIZES[i]), :] = grad[:, cols] + mem[at, cols].astype(F32)

    for copy in to_all:
        copy.wait_recv()
    total = own_list[...]
    for s in range(slots - 1):
        total = total + all_lists[s]
    head = lax.shift_right_logical(total, 12)
    row = total - head * 4096
    rows_at[...] = row
    heads_at[...] = head
    index_v[...] = head * features + row
    index_copy.start()
    index_copy.wait()

    def bent(j, n):
        return (n // 2 + ((j + 1) >> 1) * (1 - 2 * (j & 1))) & (n - 1)

    def gather(target, piece, first_row):
        @pl.loop(0, in_piece)
        def _(step):
            slot = piece * in_piece + step
            to_x = (x + bent(slot & (NX - 1), NX)) & (NX - 1)
            to_z = (z + bent(slot >> 2, NZ)) & (NZ - 1)
            start = first_row + (to_x * NZ + to_z) * share
            base = pl.multiple_of(slot * share, share)
            found = [blocks[pl.ds(index_s[0, start + u], 1), :] for u in range(share)]
            for u in range(share):
                target[pl.ds(base + u, 1), :] = found[u]

    to_core = [
        remote(peer_part.at[pl.ds(p * quarter, quarter)], from_core.at[pl.ds(p * quarter, quarter)], C + p, other)
        for p in range(pieces)
    ]
    to_chips = []
    for turn in ORDER:
        p = turn % pieces
        if turn < pieces:
            gather(peer_part, p, (1 - core) * half)
            to_core[p].start()
            continue
        gather(own_part, p, core * half)
        to_core[p].wait_recv()
        rows = slice(p * quarter, (p + 1) * quarter)
        own_part[rows, :] = own_part[rows, :] + from_core[rows, :]
        for s in range(p * in_piece, min((p + 1) * in_piece, slots - 1)):
            copy = remote(own_part.at[pl.ds(s * share, share)], from_chips.at[s], R + s, chip(*chips[s]))
            copy.start()
            to_chips.append(copy)

    head_row = lax.broadcasted_iota(I32, (columns, 1), 0) // HD
    heads[...] = jnp.where(head_row == heads_at[...], 1.0, 0.0).astype(BF16)

    size = 256

    def update(i):
        at = slice(i * size, (i + 1) * size)
        feature = lax.broadcasted_iota(I32, (size, 1), 0) + i * size
        hit = jnp.where(feature == rows_at[...], 1.0, 0.0).astype(BF16)
        unsent = 1.0 - dot(hit, heads[...], 1, 1)
        for h in range(heads_here):
            cols = slice(h * HD, (h + 1) * HD)
            error = blocks[pl.ds(h * features + i * size, size), :] * unsent[:, cols]
            stored = mem[at, cols].astype(F32)
            updated[0, at, cols] = ((1.0 - LOWPASS) * stored + LOWPASS * error).astype(BF16)

    for i in range(0, UPDATES[0]):
        update(i)

    for copy in to_chips:
        copy.wait_recv()
    mine = own_part[(slots - 1) * share : slots * share, :]
    for s in range(slots - 1):
        mine = mine + from_chips[s]

    def share_of(xx, zz):
        return summed.at[0, pl.ds(core * half + xx * quarter + zz * share, share)]

    def quarter_of(cc, xx):
        return summed.at[0, pl.ds(cc * half + xx * quarter, quarter)]

    summed[0, pl.ds(pl.multiple_of(core * half + x * quarter + z * share, share), share), :] = mine
    out = [remote(share_of(x, z), share_of(x, z), G + s, chip(dx, dz)) for s, (dx, dz) in enumerate(away)]
    done = UPDATES[0]
    for s, copy in enumerate(out):
        copy.start()
        if s in STAGGER:
            update(done)
            done += 1
    for i in range(done, features // size):
        update(i)
    to_other = []
    for dx in (0, 1, NX - 1, 2):
        from_x = lax.rem(x + NX - dx, NX)
        for s, (sx, sz) in enumerate(away):
            if sx == dx:
                back = share_of(from_x, lax.rem(z + NZ - sz, NZ))
                remote(back, back, G + s, chip(sx, sz)).wait_recv()
        copy = remote(quarter_of(core, from_x), quarter_of(core, from_x), F + dx, other)
        copy.start()
        to_other.append(copy)
    for dx in (0, 1, NX - 1, 2):
        back = quarter_of(1 - core, lax.rem(x + NX - dx, NX))
        remote(back, back, F + dx, other).wait_recv()
    for copy in to_all + to_core + to_chips + out + to_other:
        copy.wait_send()


def flush(summed, updated, summed_out, updated_out, sem):
    copies = [
        pltpu.make_async_copy(updated, updated_out, sem.at[0]),
        pltpu.make_async_copy(summed, summed_out, sem.at[1]),
    ]
    for copy in copies:
        copy.start()
    for copy in copies:
        copy.wait()


def body(tokens, upstream, memory, block_lists, leader):
    count, features = tokens.shape
    columns = upstream.shape[1]
    chosen = block_lists.shape[2]
    half = chosen // 2
    quarter = half // NX
    share = quarter // NZ
    hbm = pl.BlockSpec(memory_space=pltpu.HBM)
    vmem = pl.BlockSpec(memory_space=pltpu.VMEM)
    copies = 3 * (NX * NZ - 1) + 9
    summed, updated = pl.pallas_call(
        kernel,
        out_shape=(
            pltpu.VMEM((1, chosen, HD), F32),
            pltpu.VMEM((1, features, columns), BF16),
        ),
        in_specs=[hbm, hbm, hbm, hbm, pl.BlockSpec(memory_space=pltpu.SMEM)],
        out_specs=(vmem, vmem),
        scratch_shapes=[
            pltpu.VMEM((count, features), BF16),
            pltpu.VMEM((count, columns), BF16),
            pltpu.VMEM((features, columns), BF16),
            pltpu.VMEM((features * columns // HD, HD), F32),
            pltpu.VMEM((columns, chosen), BF16),
            pltpu.VMEM((1, chosen), I32),
            pltpu.VMEM((1, chosen), I32),
            pltpu.VMEM((1, chosen), I32),
            pltpu.VMEM((NX * NZ - 1, 1, chosen), I32),
            pltpu.VMEM((1, chosen), I32),
            pltpu.VMEM((1, chosen), I32),
            pltpu.VMEM((1, chosen), I32),
            pltpu.SMEM((1, chosen), I32),
            pltpu.VMEM((half, HD), F32),
            pltpu.VMEM((half, HD), F32),
            pltpu.VMEM((half, HD), F32),
            pltpu.VMEM((NX * NZ - 1, share, HD), F32),
            pltpu.SemaphoreType.DMA((1 + 2 * len(SIZES),)),
            pltpu.SemaphoreType.DMA((2,)),
            pltpu.SemaphoreType.DMA((copies,)),
            pltpu.SemaphoreType.DMA((copies,)),
        ],
        compiler_params=pltpu.CompilerParams(
            collective_id=0, has_side_effects=True, vmem_limit_bytes=VMEM_MIB * 2**20
        ),
        name="scalecom",
    )(*(pltpu.with_memory_space_constraint(a, pltpu.HBM) for a in (tokens, upstream, memory, block_lists[0])), leader)
    return pl.pallas_call(
        flush,
        out_shape=(
            jax.ShapeDtypeStruct(summed.shape, F32),
            jax.ShapeDtypeStruct(updated.shape, BF16),
        ),
        in_specs=[vmem, vmem],
        out_specs=(hbm, hbm),
        scratch_shapes=[pltpu.SemaphoreType.DMA((2,))],
        compiler_params=pltpu.CompilerParams(vmem_limit_bytes=2**20),
        name="flush",
    )(*(pltpu.with_memory_space_constraint(a, pltpu.VMEM) for a in (summed, updated)))


def solution(mesh):
    placed = (
        P("dp", None),
        P("dp", "tensor"),
        P("dp", None, "tensor"),
        P("dp", "tensor", None),
        P(),
    )
    return jax.shard_map(
        body,
        mesh=mesh,
        in_specs=placed,
        out_specs=(P("tensor", None, None), P("dp", None, "tensor")),
        check_vma=False,
    )
```

```python
import functools

import jax
import jax.numpy as jnp
from jax import lax
from jax.experimental import pallas as pl
from jax.experimental.pallas import tpu as pltpu
from jax.sharding import PartitionSpec as P

HD = 128
LOWPASS = 0.3
VMEM_MIB = 40
SIZES = (512, 512, 512, 512, 512)
LIST_AT = 1
ORDER = (0, 1, 4, 2, 5, 3, 6, 7)
UPDATES = (6, 4)
STAGGER = ()
NX, NZ = 4, 8
F32, BF16, I32 = jnp.float32, jnp.bfloat16, jnp.int32
MESH = pl.DeviceIdType.MESH


def dot(a, b, ca, cb):
    return lax.dot_general(a, b, (((ca,), (cb,)), ((), ())), preferred_element_type=F32)


def far_first():
    zs = [(NZ // 2 + (j + 1) // 2 * (1 - 2 * (j % 2))) % NZ for j in range(NZ)]
    xs = [(NX // 2 + (j + 1) // 2 * (1 - 2 * (j % 2))) % NX for j in range(NX)]
    return [(dx, dz) for dz in zs for dx in xs]


def kernel(
    tokens, upstream, memory, lists, leader, summed, updated,
    tok, up, mem, blocks, heads, own_list, lone, peer_list, all_lists, rows_at, heads_at, index_v, index_s,
    peer_part, own_part, from_core, from_chips,
    load_sem, index_sem, send_sem, recv_sem,
):
    features = tokens.shape[1]
    columns = upstream.shape[1]
    heads_here = columns // HD
    chosen = lists.shape[1]
    half, quarter, share = chosen // 2, chosen // 2 // NX, chosen // 2 // NX // NZ
    offsets = [sum(SIZES[:i]) for i in range(len(SIZES))]
    chunks = len(SIZES)
    slots = NX * NZ
    chips = far_first()
    away = chips[:-1]

    me = lax.axis_index("dp")
    core = lax.rem(me, 2)
    z = lax.rem(me // 2, NZ)
    x = me // (2 * NZ)
    other = {"dp": me + 1 - 2 * core}

    def chip(dx, dz):
        return {"dp": (lax.rem(x + dx, NX) * NZ + lax.rem(z + dz, NZ)) * 2 + core}

    def remote(src, dst, at, device):
        return pltpu.make_async_remote_copy(
            src_ref=src, dst_ref=dst, send_sem=send_sem.at[at], recv_sem=recv_sem.at[at],
            device_id=device, device_id_type=MESH,
        )

    pieces = 4
    in_piece = slots // pieces
    L1, L2 = 0, 1
    C = L2 + slots - 1
    R = C + pieces
    G = R + slots - 1
    F = G + slots - 1

    barrier = pltpu.get_barrier_semaphore()
    load_list = pltpu.make_async_copy(lists, own_list, index_sem.at[1])
    load_list.start()
    load_up = pltpu.make_async_copy(upstream, up, load_sem.at[0])
    load_up.start()
    loads, keeps = [], []
    for i in range(chunks):
        at = pl.ds(offsets[i], SIZES[i])
        loads.append(pltpu.make_async_copy(tokens.at[:, at], tok.at[:, at], load_sem.at[1 + 2 * i]))
        keeps.append(pltpu.make_async_copy(memory.at[0, at], mem.at[at], load_sem.at[2 + 2 * i]))

    loads[0].start()
    keeps[0].start()
    for dx, dz in away:
        pl.semaphore_signal(barrier, inc=1, device_id=chip(dx, dz), device_id_type=MESH)
    pl.semaphore_signal(barrier, inc=1, device_id=other, device_id_type=MESH)

    load_list.wait()
    block = own_list[...]
    row = lax.shift_right_logical(block * 52429, 18)
    code = (block - row * heads_here) * 4096 + row
    lone[...] = code * jnp.where(leader[0] == me, 1, 0)

    to_peer = remote(lone, peer_list, L1, other)
    to_all = [remote(own_list, all_lists.at[s], L2 + s, chip(dx, dz)) for s, (dx, dz) in enumerate(away)]
    index_copy = pltpu.make_async_copy(index_v, index_s, index_sem.at[0])

    for i in range(chunks):
        if i == LIST_AT:
            pl.semaphore_wait(barrier, slots)
            to_peer.start()
            to_peer.wait()
            own_list[...] = lone[...] + peer_list[...]
            for copy in to_all:
                copy.start()
        if i == 0:
            load_up.wait()
        loads[i].wait()
        keeps[i].wait()
        if i + 1 < chunks:
            loads[i + 1].start()
            keeps[i + 1].start()
        at = slice(offsets[i], offsets[i] + SIZES[i])
        grad = dot(tok[:, at], up[...], 0, 0)
        for h in range(heads_here):
            cols = slice(h * HD, (h + 1) * HD)
            blocks[pl.ds(h * features + offsets[i], SIZES[i]), :] = grad[:, cols] + mem[at, cols].astype(F32)

    for copy in to_all:
        copy.wait_recv()
    total = own_list[...]
    for s in range(slots - 1):
        total = total + all_lists[s]
    head = lax.shift_right_logical(total, 12)
    row = total - head * 4096
    rows_at[...] = row
    heads_at[...] = head
    index_v[...] = head * features + row
    index_copy.start()
    index_copy.wait()

    def bent(j, n):
        return (n // 2 + ((j + 1) >> 1) * (1 - 2 * (j & 1))) & (n - 1)

    def gather(target, piece, first_row):
        @pl.loop(0, in_piece, unroll=2)
        def _(step):
            slot = piece * in_piece + step
            to_x = (x + bent(slot & (NX - 1), NX)) & (NX - 1)
            to_z = (z + bent(slot >> 2, NZ)) & (NZ - 1)
            start = first_row + (to_x * NZ + to_z) * share
            base = pl.multiple_of(slot * share, share)
            found = [blocks[pl.ds(index_s[0, start + u], 1), :] for u in range(share)]
            for u in range(share):
                target[pl.ds(base + u, 1), :] = found[u]

    to_core = [
        remote(peer_part.at[pl.ds(p * quarter, quarter)], from_core.at[pl.ds(p * quarter, quarter)], C + p, other)
        for p in range(pieces)
    ]
    to_chips = []
    for turn in ORDER:
        p = turn % pieces
        if turn < pieces:
            gather(peer_part, p, (1 - core) * half)
            to_core[p].start()
            continue
        gather(own_part, p, core * half)
        to_core[p].wait_recv()
        rows = slice(p * quarter, (p + 1) * quarter)
        own_part[rows, :] = own_part[rows, :] + from_core[rows, :]
        for s in range(p * in_piece, min((p + 1) * in_piece, slots - 1)):
            copy = remote(own_part.at[pl.ds(s * share, share)], from_chips.at[s], R + s, chip(*chips[s]))
            copy.start()
            to_chips.append(copy)

    head_row = lax.broadcasted_iota(I32, (columns, 1), 0) // HD
    heads[...] = jnp.where(head_row == heads_at[...], 1.0, 0.0).astype(BF16)

    size = 256

    def update(i):
        at = slice(i * size, (i + 1) * size)
        feature = lax.broadcasted_iota(I32, (size, 1), 0) + i * size
        hit = jnp.where(feature == rows_at[...], 1.0, 0.0).astype(BF16)
        unsent = 1.0 - dot(hit, heads[...], 1, 1)
        for h in range(heads_here):
            cols = slice(h * HD, (h + 1) * HD)
            error = blocks[pl.ds(h * features + i * size, size), :] * unsent[:, cols]
            stored = mem[at, cols].astype(F32)
            updated[0, at, cols] = ((1.0 - LOWPASS) * stored + LOWPASS * error).astype(BF16)

    for i in range(0, UPDATES[0]):
        update(i)

    for copy in to_chips:
        copy.wait_recv()
    mine = own_part[(slots - 1) * share : slots * share, :]
    for s in range(slots - 1):
        mine = mine + from_chips[s]

    def share_of(xx, zz):
        return summed.at[0, pl.ds(core * half + xx * quarter + zz * share, share)]

    def quarter_of(cc, xx):
        return summed.at[0, pl.ds(cc * half + xx * quarter, quarter)]

    summed[0, pl.ds(pl.multiple_of(core * half + x * quarter + z * share, share), share), :] = mine
    out = [remote(share_of(x, z), share_of(x, z), G + s, chip(dx, dz)) for s, (dx, dz) in enumerate(away)]
    done = UPDATES[0]
    for s, copy in enumerate(out):
        copy.start()
        if s in STAGGER:
            update(done)
            done += 1
    for i in range(done, features // size):
        update(i)
    to_other = []
    for dx in (0, 1, NX - 1, 2):
        from_x = lax.rem(x + NX - dx, NX)
        for s, (sx, sz) in enumerate(away):
            if sx == dx:
                back = share_of(from_x, lax.rem(z + NZ - sz, NZ))
                remote(back, back, G + s, chip(sx, sz)).wait_recv()
        copy = remote(quarter_of(core, from_x), quarter_of(core, from_x), F + dx, other)
        copy.start()
        to_other.append(copy)
    for dx in (0, 1, NX - 1, 2):
        back = quarter_of(1 - core, lax.rem(x + NX - dx, NX))
        remote(back, back, F + dx, other).wait_recv()
    for copy in to_all + to_core + to_chips + out + to_other:
        copy.wait_send()


def flush(summed, updated, summed_out, updated_out, sem):
    copies = [
        pltpu.make_async_copy(updated, updated_out, sem.at[0]),
        pltpu.make_async_copy(summed, summed_out, sem.at[1]),
    ]
    for copy in copies:
        copy.start()
    for copy in copies:
        copy.wait()


def body(tokens, upstream, memory, block_lists, leader):
    count, features = tokens.shape
    columns = upstream.shape[1]
    chosen = block_lists.shape[2]
    half = chosen // 2
    quarter = half // NX
    share = quarter // NZ
    hbm = pl.BlockSpec(memory_space=pltpu.HBM)
    vmem = pl.BlockSpec(memory_space=pltpu.VMEM)
    copies = 3 * (NX * NZ - 1) + 9
    summed, updated = pl.pallas_call(
        kernel,
        out_shape=(
            pltpu.VMEM((1, chosen, HD), F32),
            pltpu.VMEM((1, features, columns), BF16),
        ),
        in_specs=[hbm, hbm, hbm, hbm, pl.BlockSpec(memory_space=pltpu.SMEM)],
        out_specs=(vmem, vmem),
        scratch_shapes=[
            pltpu.VMEM((count, features), BF16),
            pltpu.VMEM((count, columns), BF16),
            pltpu.VMEM((features, columns), BF16),
            pltpu.VMEM((features * columns // HD, HD), F32),
            pltpu.VMEM((columns, chosen), BF16),
            pltpu.VMEM((1, chosen), I32),
            pltpu.VMEM((1, chosen), I32),
            pltpu.VMEM((1, chosen), I32),
            pltpu.VMEM((NX * NZ - 1, 1, chosen), I32),
            pltpu.VMEM((1, chosen), I32),
            pltpu.VMEM((1, chosen), I32),
            pltpu.VMEM((1, chosen), I32),
            pltpu.SMEM((1, chosen), I32),
            pltpu.VMEM((half, HD), F32),
            pltpu.VMEM((half, HD), F32),
            pltpu.VMEM((half, HD), F32),
            pltpu.VMEM((NX * NZ - 1, share, HD), F32),
            pltpu.SemaphoreType.DMA((1 + 2 * len(SIZES),)),
            pltpu.SemaphoreType.DMA((2,)),
            pltpu.SemaphoreType.DMA((copies,)),
            pltpu.SemaphoreType.DMA((copies,)),
        ],
        compiler_params=pltpu.CompilerParams(
            collective_id=0, has_side_effects=True, vmem_limit_bytes=VMEM_MIB * 2**20
        ),
        name="scalecom",
    )(*(pltpu.with_memory_space_constraint(a, pltpu.HBM) for a in (tokens, upstream, memory, block_lists[0])), leader)
    return pl.pallas_call(
        flush,
        out_shape=(
            jax.ShapeDtypeStruct(summed.shape, F32),
            jax.ShapeDtypeStruct(updated.shape, BF16),
        ),
        in_specs=[vmem, vmem],
        out_specs=(hbm, hbm),
        scratch_shapes=[pltpu.SemaphoreType.DMA((2,))],
        compiler_params=pltpu.CompilerParams(vmem_limit_bytes=2**20),
        name="flush",
    )(*(pltpu.with_memory_space_constraint(a, pltpu.VMEM) for a in (summed, updated)))


def solution(mesh):
    placed = (
        P("dp", None),
        P("dp", "tensor"),
        P("dp", None, "tensor"),
        P("dp", "tensor", None),
        P(),
    )
    return jax.shard_map(
        body,
        mesh=mesh,
        in_specs=placed,
        out_specs=(P("tensor", None, None), P("dp", None, "tensor")),
        check_vma=False,
    )
```
